32 devices in a mesh: group: 2 (over x), atom: 4 (over y, core), layer: 4 (over z).
Axes of the slice: x: 2, y: 2, z: 4, core: 2. Of those that a mesh axis runs over, the one named last changes fastest.
Arguments:
- activations: bfloat16 [256, 4, 2304], P('group', 'layer'), parts along dimension 0, may hold values from -6 to 6
- encoder: bfloat16 [8, 2304, 16384], P(('group', 'layer'), None, 'atom'), parts along dimension 0, may hold values from -0.0625 to 0.0625
- decoder: bfloat16 [32768, 4, 2304], P(('group', 'atom'), 'layer'), parts along dimension 0, may hold values from -1 to 1
- thresholds: float32 [32768], P(('group', 'atom')), parts along dimension 0, may hold values from 0.05 to 0.8
Outputs:
- codes: bfloat16 [256, 16384], P('group', 'atom'), parts along dimension 0
- reconstruction: bfloat16 [256, 4, 2304], P(('group', 'atom'), 'layer'), parts along dimension 0
The draws below stay inside these ranges and needn't reach their ends.
There are 2 independent parts, one for each index of `group`. The reference program is written for one: setup_inputs(seed, part) draws one part's arguments, and reference() takes and returns one part's arrays. A program takes and returns all parts, laid end to end along the dimension named above; each array names one. Nothing has to cross between parts.
All inputs are finite; a program needn't handle non-finite values.
Results may differ from the reference program's by a relative error of at most 0.02.
The reference program's roundings to bfloat16 on the way count: a program that leaves them out, or rounds other values in their place, can miss the bound.
Values may be sent and summed in bfloat16 or wider, within the bound.
A program may use at most 128 MiB of HBM per device.

```python
import math
import jax
import jax.numpy as jnp
from jax import lax

D = 2304
ATOMS = 16384
LAYERS = 4
TOKENS = 128
REFINES = 2
N_ATOM = 4


def draw_activations(key, part):
    subkeys = jax.random.split(jax.random.fold_in(key, 23), 1)
    array_shape = (TOKENS, LAYERS, D)
    values = jax.random.truncated_normal(subkeys[0], -6.0, 6.0, array_shape, jnp.float32)
    return values.astype(jnp.bfloat16)


def draw_decoder(key, part):
    subkeys = jax.random.split(jax.random.fold_in(key, 11), 2)
    array_shape = (ATOMS, LAYERS, D)
    base_draw = jax.random.truncated_normal(subkeys[0], -4.0, 4.0, array_shape, jnp.float32)
    layer_gain = 0.5 + jnp.arange(LAYERS, dtype=jnp.float32) / max(LAYERS - 1, 1)
    atom_gain = jnp.exp(jax.random.uniform(subkeys[1], (ATOMS, 1, 1), jnp.float32, math.log(0.75), math.log(1.33)))
    scale_now = math.sqrt(5.0) / (math.sqrt(ATOMS) + math.sqrt(LAYERS * D))
    values = base_draw * layer_gain[None, :, None] * atom_gain * scale_now
    return values.astype(jnp.bfloat16)


def steps_of(key, extent, pieces, least, largest):
    def one(dim, parts):
        heights = jax.random.uniform(jax.random.fold_in(jax.random.fold_in(key, 6), dim), (parts,), jnp.float32, least / len(pieces), largest / len(pieces))
        return jnp.repeat(jnp.exp(heights), extent[dim] // parts).reshape((-1,) + (1,) * (len(extent) - dim - 1))

    factor_of = one(*pieces[0])
    for cut in pieces[1:]:
        factor_of = factor_of * one(*cut)
    return factor_of


def centred(own_key, dims, width, reach, shards=(), held_as=jnp.bfloat16):
    factor_of = steps_of(own_key, dims, shards, -0.22, 0.18) if shards else 1.0
    result = jax.random.normal(own_key, dims, jnp.float32) * width * factor_of
    return jnp.minimum(jnp.maximum(result, -reach), reach).astype(held_as)


def setup_inputs(seed: int = 0, part: int = 0) -> dict:
    streams_of = jax.random.split(jax.random.key(seed), 5)
    own_keys = jax.random.split(jax.random.fold_in(streams_of[4], part), 5)
    activations = draw_activations(jax.random.fold_in(jax.random.fold_in(streams_of[4], part), 71), part)
    encoder = centred(own_keys[1], (LAYERS, D, ATOMS), (LAYERS * D) ** -0.5, 0.0625, ((0, 4), (2, 4)))
    decoder = draw_decoder(jax.random.fold_in(jax.random.fold_in(streams_of[4], part), 71), part)
    thresholds = jnp.clip(jnp.exp(math.log(0.8) - 2.7725887 * jax.random.uniform(own_keys[3], (ATOMS,), jnp.float32) ** steps_of(own_keys[3], (ATOMS,), ((0, 4),), -0.2, 0.2)), 0.05, 0.8)
    return {"activations": activations, "encoder": encoder, "decoder": decoder, "thresholds": thresholds}


step_rate = 0.15
learn_rate = 0.001

def rounded(value):
    return lax.optimization_barrier(value.astype(jnp.bfloat16)).astype(jnp.float32)

def rebuild(coded_now, weights):
    atom_width = ATOMS // N_ATOM
    summed = jnp.zeros((TOKENS, LAYERS * D), jnp.float32)
    for shard_index in range(N_ATOM):
        column_block = coded_now[:, shard_index * atom_width:(shard_index + 1) * atom_width]
        dec_table = weights[shard_index * atom_width:(shard_index + 1) * atom_width].reshape(atom_width, LAYERS * D)
        summed = summed + rounded(jnp.dot(column_block, dec_table, preferred_element_type=jnp.float32))
    return summed.reshape(TOKENS, LAYERS, D)

def code_grad(residual, weights):
    summed = jnp.zeros((TOKENS, ATOMS), jnp.float32)
    for layer_index in range(LAYERS):
        summed = summed + rounded(jnp.dot(residual[:, layer_index], weights[:, layer_index].T, preferred_element_type=jnp.float32))
    return summed

def make_residual(acts_wide, coded_now, weights):
    return (acts_wide - rebuild(coded_now, weights)).astype(jnp.bfloat16)

def refine(acts_wide, code_state, coded_now, weights, thresholds):
    residual = make_residual(acts_wide, coded_now, weights)
    gradient = code_grad(residual, weights)
    code_state = jax.nn.relu(code_state + step_rate * gradient - step_rate * thresholds)
    return (code_state, code_state.astype(jnp.bfloat16))

def reference(activations, encoder, decoder, thresholds):
    acts_wide = activations.astype(jnp.float32)
    preact = jnp.zeros((TOKENS, ATOMS), jnp.float32)
    for layer_index in range(LAYERS):
        preact = preact + rounded(jnp.dot(activations[:, layer_index], encoder[layer_index], preferred_element_type=jnp.float32))
    code_state = jax.nn.relu(preact - thresholds)
    coded_now = code_state.astype(jnp.bfloat16)
    for sweep in range(REFINES):
        code_state, coded_now = refine(acts_wide, code_state, coded_now, decoder, thresholds)
    residual = make_residual(acts_wide, coded_now, decoder)
    update = jnp.stack([jnp.dot(coded_now.T, residual[:, layer_index], preferred_element_type=jnp.float32) for layer_index in range(LAYERS)], axis=1)
    renewed = (decoder.astype(jnp.float32) + learn_rate * (update / TOKENS)).astype(jnp.bfloat16)
    code_state, coded_now = refine(acts_wide, code_state, coded_now, renewed, thresholds)
    reconstruction = rebuild(coded_now, renewed).astype(jnp.bfloat16)
    return (coded_now, reconstruction)
```

```python
import functools

import jax
import jax.numpy as jnp
from jax import lax
from jax.experimental import pallas as pl
from jax.experimental.pallas import tpu as pltpu
from jax.sharding import PartitionSpec as P

REFINES = 2


step_rate = 0.15
learn_rate = 0.001


def shards(activations, encoder, decoder, thresholds):
    rows_in = activations[:, 0, :]
    enc_local = encoder[0]
    dec_local = decoder[:, 0, :]
    tokens = rows_in.shape[0]
    atom_devices = lax.axis_size("atom")

    def spread(code_state):
        return code_state.astype(jnp.bfloat16)

    def residual_of(coded_now, weights):
        row_count = tokens // atom_devices
        partial_value = lax.psum_scatter(
            jnp.dot(coded_now, weights, preferred_element_type=jnp.float32).astype(jnp.bfloat16),
            "atom",
            scatter_dimension=0,
            tiled=True,
        ).astype(jnp.float32)
        own_rows = lax.dynamic_slice_in_dim(
            rows_in, lax.axis_index("atom") * row_count, row_count, 0
        ).astype(jnp.float32)
        residual = lax.all_gather(
            (own_rows - partial_value).astype(jnp.bfloat16), "atom", axis=0, tiled=True
        )
        return (residual, False)

    def refine(code_state, coded_now, weights):
        residual, transposed = residual_of(coded_now, weights)
        gradient = lax.psum(
            lax.dot_general(
                residual, weights, (((1,), (1,)), ((), ())), preferred_element_type=jnp.float32
            ).astype(jnp.bfloat16),
            "layer",
        ).astype(jnp.float32)
        code_state = jax.nn.relu(code_state + step_rate * gradient - step_rate * thresholds)
        return (code_state, spread(code_state))

    preact = lax.psum(
        jnp.dot(rows_in, enc_local, preferred_element_type=jnp.float32).astype(jnp.bfloat16),
        "layer",
    ).astype(jnp.float32)
    code_state = jax.nn.relu(preact - thresholds)
    coded_now = spread(code_state)
    for sweep in range(REFINES):
        code_state, coded_now = refine(code_state, coded_now, dec_local)
    residual, transposed = residual_of(coded_now, dec_local)
    update = lax.dot_general(
        coded_now, residual, (((0,), (0,)), ((), ())), preferred_element_type=jnp.float32
    )
    renewed = (dec_local.astype(jnp.float32) + learn_rate * (update / tokens)).astype(jnp.bfloat16)
    code_state, coded_now = refine(code_state, coded_now, renewed)
    rebuilt = lax.psum_scatter(
        jnp.dot(coded_now, renewed, preferred_element_type=jnp.float32).astype(jnp.bfloat16),
        "atom",
        scatter_dimension=0,
        tiled=True,
    )
    reconstruction = rebuilt[:, None, :]
    return (coded_now, reconstruction)


MESH = pl.DeviceIdType.MESH
WIDE = 256
LAG = (2, 4, 6, 8)


def dot(a, b, dims):
    return lax.dot_general(a, b, (dims, ((), ())), preferred_element_type=jnp.float32)


def wide(x):
    return x.astype(jnp.float32)


def fused(chunks, tokens, acts, enc_hbm, dec_hbm, thr, codes_out, recon_out,
          enc, dec, own, ends, parts, coded, state, acc, res, terms, core_in, y_out, y_in,
          enc_sem, dec_sem, end_s, end_r, part_s, part_r, code_s, code_s2, code_r,
          a_s, a_r):
    z = lax.axis_index("layer")
    a = lax.axis_index("atom")
    rows = tokens // 4
    core, y = lax.rem(a, 2), a // 2
    mate = a + 1 - 2 * core
    across = lax.rem(a + 2, 4)
    diagonal = lax.rem(mate + 2, 4)
    is_mid = z * (3 - z) != 0
    is_end = z * (3 - z) == 0

    def load_enc(c):
        return pltpu.make_async_copy(
            enc_hbm.at[:, pl.ds(pl.multiple_of(c * WIDE, WIDE), WIDE)], enc.at[c], enc_sem.at[c])

    def load_dec(c):
        return pltpu.make_async_copy(dec_hbm.at[c], dec.at[c], dec_sem.at[c])

    @pl.loop(0, chunks)
    def _(c):
        load_enc(c).start()

    @pl.loop(0, chunks)
    def _(c):
        load_dec(c).start()

    barrier = pltpu.get_barrier_semaphore()
    for step in (1, 2, 3):
        pl.semaphore_signal(barrier, inc=1, device_id={"layer": lax.rem(z + step, 4)}, device_id_type=MESH)
    for peer in (mate, across):
        pl.semaphore_signal(barrier, inc=1, device_id={"atom": peer}, device_id_type=MESH)
    pl.semaphore_wait(barrier, 5)

    def to_layer(src, dst, send, recv, layer):
        return pltpu.make_async_remote_copy(
            src, dst, send, recv, device_id={"layer": layer}, device_id_type=MESH)

    def to_atom(src, dst, k, atom):
        return pltpu.make_async_remote_copy(
            src, dst, a_s.at[k], a_r.at[k], device_id={"atom": atom}, device_id_type=MESH)

    inner = 1 + z // 3
    outer = 3 * (z - 1)
    other = 3 - z

    def end_copy(c):
        return to_layer(own.at[c], ends.at[c], end_s.at[c], end_r.at[c], inner)

    def part_copy(c):
        return to_layer(own.at[c], parts.at[c], part_s.at[c], part_r.at[c], other)

    def code_out(c):
        return to_layer(coded.at[c], coded.at[c], code_s.at[c], code_r.at[c], outer)

    def code_over(c):
        return to_layer(coded.at[c], coded.at[c], code_s2.at[c], code_r.at[c], other)

    def layer_phase(term, finish, first):
        acc[...] = jnp.zeros_like(acc)

        @pl.loop(0, chunks + LAG[3])
        def _(s):
            @pl.when(s < chunks)
            def _():
                own[s] = term(s).astype(jnp.bfloat16)

                @pl.when(is_end)
                def _():
                    end_copy(s).start()

            c1 = s - LAG[0]

            @pl.when(is_mid & (c1 >= 0) & (c1 < chunks))
            def _():
                end_copy(c1).wait_recv()

                @pl.when(z == 2 - lax.rem(c1, 2))
                def _():
                    own[c1] = (wide(own[c1]) + wide(ends[c1])).astype(jnp.bfloat16)
                    part_copy(c1).start()

            c2 = s - LAG[1]

            @pl.when((c2 >= 0) & (c2 < chunks))
            def _():
                @pl.when(z == 1 + lax.rem(c2, 2))
                def _():
                    part_copy(c2).wait_recv()
                    now = finish(c2, wide(own[c2]) + wide(ends[c2]) + wide(parts[c2]))
                    state[c2] = now
                    coded[c2] = now.astype(jnp.bfloat16)
                    code_over(c2).start()
                    code_out(c2).start()

            c3 = s - LAG[2]

            @pl.when((c3 >= 0) & (c3 < chunks))
            def _():
                @pl.when(z == 2 - lax.rem(c3, 2))
                def _():
                    code_over(c3).wait_recv()
                    code_out(c3).start()

            c4 = s - LAG[3]

            @pl.when(c4 >= 0)
            def _():
                @pl.when(is_end)
                def _():
                    code_out(c4).wait_recv()

                if first:
                    load_dec(c4).wait()
                acc[...] += dot(coded[c4], dec[c4], ((1,), (0,)))

        @pl.loop(0, chunks)
        def _(c):
            @pl.when(is_end)
            def _():
                end_copy(c).wait_send()

            @pl.when(is_mid)
            def _():
                code_out(c).wait_send()

            @pl.when(z == 2 - lax.rem(c, 2))
            def _():
                part_copy(c).wait_send()

            @pl.when(z == 1 + lax.rem(c, 2))
            def _():
                code_over(c).wait_send()

    def block(r):
        return pl.ds(pl.multiple_of(r * rows, rows), rows)

    def atom_sum():
        for r in range(4):
            terms[r] = acc[r * rows:(r + 1) * rows].astype(jnp.bfloat16)
        far = to_atom(terms.at[2 * (1 - y) + 1 - core], core_in.at[0], 0, mate)
        near = to_atom(terms.at[2 * y + 1 - core], core_in.at[1], 1, mate)
        far.start()
        near.start()
        far.wait_recv()
        y_out[...] = (wide(terms[2 * (1 - y) + core]) + wide(core_in[0])).astype(jnp.bfloat16)
        over = to_atom(y_out, y_in, 2, across)
        over.start()
        near.wait_recv()
        over.wait_recv()
        total = wide(terms[2 * y + core]) + wide(core_in[1]) + wide(y_in[...])
        far.wait_send()
        near.wait_send()
        over.wait_send()
        return total

    def atom_stage():
        total = atom_sum()
        res[block(a)] = (wide(acts[block(a)]) - total).astype(jnp.bfloat16)
        over = to_atom(res.at[block(a)], res.at[block(a)], 3, across)
        near = to_atom(res.at[block(a)], res.at[block(a)], 4, mate)
        far = to_atom(res.at[block(across)], res.at[block(across)], 5, mate)
        over.start()
        near.start()
        over.wait_recv()
        far.start()
        near.wait_recv()
        far.wait_recv()
        over.wait_send()
        near.wait_send()
        far.wait_send()

    def encode(c):
        load_enc(c).wait()
        return dot(acts[...], enc[c], ((1,), (0,)))

    layer_phase(encode, lambda c, total: jnp.maximum(total - thr[c], 0.0), True)

    def renew():
        acc[...] = jnp.zeros_like(acc)

        @pl.loop(0, chunks)
        def _(c):
            update = dot(coded[c], res[...], ((0,), (0,)))
            dec[c] = (wide(dec[c]) + learn_rate * (update / tokens)).astype(jnp.bfloat16)
            acc[...] += dot(coded[c], dec[c], ((1,), (0,)))

    @pl.loop(0, REFINES + 2)
    def _(p):
        atom_stage()

        @pl.when(p == REFINES)
        def _():
            renew()

        @pl.when(p != REFINES)
        def _():
            layer_phase(
                lambda c: dot(res[...], dec[c], ((1,), (1,))),
                lambda c, total: jnp.maximum(
                    state[c] + step_rate * total - step_rate * thr[c], 0.0),
                False,
            )

    for c in range(chunks):
        codes_out[:, c * WIDE:(c + 1) * WIDE] = coded[c]
    recon_out[...] = atom_sum().astype(jnp.bfloat16)


def fused_shards(activations, encoder, decoder, thresholds):
    tokens, _, width = activations.shape
    atoms = decoder.shape[0]
    chunks = atoms // WIDE
    rows = tokens // 4
    bf16, f32 = jnp.bfloat16, jnp.float32
    vmem = pl.BlockSpec(memory_space=pltpu.VMEM)
    hbm = pl.BlockSpec(memory_space=pltpu.HBM)
    dma = pltpu.SemaphoreType.DMA
    codes, recon = pl.pallas_call(
        functools.partial(fused, chunks, tokens),
        out_shape=(
            jax.ShapeDtypeStruct((tokens, atoms), bf16),
            jax.ShapeDtypeStruct((rows, width), bf16),
        ),
        in_specs=[vmem, hbm, hbm, vmem],
        out_specs=(vmem, vmem),
        scratch_shapes=[
            pltpu.VMEM((chunks, width, WIDE), bf16),
            pltpu.VMEM((chunks, WIDE, width), bf16),
            pltpu.VMEM((chunks, tokens, WIDE), bf16),
            pltpu.VMEM((chunks, tokens, WIDE), bf16),
            pltpu.VMEM((chunks, tokens, WIDE), bf16),
            pltpu.VMEM((chunks, tokens, WIDE), bf16),
            pltpu.VMEM((chunks, tokens, WIDE), f32),
            pltpu.VMEM((tokens, width), f32),
            pltpu.VMEM((tokens, width), bf16),
            pltpu.VMEM((4, rows, width), bf16),
            pltpu.VMEM((2, rows, width), bf16),
            pltpu.VMEM((rows, width), bf16),
            pltpu.VMEM((rows, width), bf16),
        ] + [dma((chunks,))] * 9 + [dma((6,)), dma((6,))],
        compiler_params=pltpu.CompilerParams(
            collective_id=1, has_side_effects=True, vmem_limit_bytes=60 << 20),
        cost_estimate=pl.CostEstimate(
            flops=20 * tokens * atoms * width, bytes_accessed=4 * atoms * width, transcendentals=0),
        name="crosscoder",
    )(
        activations[:, 0, :],
        encoder[0],
        decoder.reshape(chunks, WIDE, width),
        thresholds.reshape(chunks, 1, WIDE),
    )
    return codes, recon[:, None, :]


def solution(mesh):
    fits = mesh.shape["atom"] == 4 and mesh.shape["layer"] == 4
    return jax.shard_map(
        fused_shards if fits else shards,
        mesh=mesh,
        in_specs=(
            P("group", "layer", None),
            P(("group", "layer"), None, "atom"),
            P(("group", "atom"), "layer", None),
            P(("group", "atom")),
        ),
        out_specs=(P("group", "atom"), P(("group", "atom"), "layer", None)),
        check_vma=False,
    )
```

```python
import functools

import jax
import jax.numpy as jnp
from jax import lax
from jax.experimental import pallas as pl
from jax.experimental.pallas import tpu as pltpu
from jax.sharding import PartitionSpec as P

REFINES = 2


step_rate = 0.15
learn_rate = 0.001


def shards(activations, encoder, decoder, thresholds):
    rows_in = activations[:, 0, :]
    enc_local = encoder[0]
    dec_local = decoder[:, 0, :]
    tokens = rows_in.shape[0]
    atom_devices = lax.axis_size("atom")

    def spread(code_state):
        return code_state.astype(jnp.bfloat16)

    def residual_of(coded_now, weights):
        row_count = tokens // atom_devices
        partial_value = lax.psum_scatter(
            jnp.dot(coded_now, weights, preferred_element_type=jnp.float32).astype(jnp.bfloat16),
            "atom",
            scatter_dimension=0,
            tiled=True,
        ).astype(jnp.float32)
        own_rows = lax.dynamic_slice_in_dim(
            rows_in, lax.axis_index("atom") * row_count, row_count, 0
        ).astype(jnp.float32)
        residual = lax.all_gather(
            (own_rows - partial_value).astype(jnp.bfloat16), "atom", axis=0, tiled=True
        )
        return (residual, False)

    def refine(code_state, coded_now, weights):
        residual, transposed = residual_of(coded_now, weights)
        gradient = lax.psum(
            lax.dot_general(
                residual, weights, (((1,), (1,)), ((), ())), preferred_element_type=jnp.float32
            ).astype(jnp.bfloat16),
            "layer",
        ).astype(jnp.float32)
        code_state = jax.nn.relu(code_state + step_rate * gradient - step_rate * thresholds)
        return (code_state, spread(code_state))

    preact = lax.psum(
        jnp.dot(rows_in, enc_local, preferred_element_type=jnp.float32).astype(jnp.bfloat16),
        "layer",
    ).astype(jnp.float32)
    code_state = jax.nn.relu(preact - thresholds)
    coded_now = spread(code_state)
    for sweep in range(REFINES):
        code_state, coded_now = refine(code_state, coded_now, dec_local)
    residual, transposed = residual_of(coded_now, dec_local)
    update = lax.dot_general(
        coded_now, residual, (((0,), (0,)), ((), ())), preferred_element_type=jnp.float32
    )
    renewed = (dec_local.astype(jnp.float32) + learn_rate * (update / tokens)).astype(jnp.bfloat16)
    code_state, coded_now = refine(code_state, coded_now, renewed)
    rebuilt = lax.psum_scatter(
        jnp.dot(coded_now, renewed, preferred_element_type=jnp.float32).astype(jnp.bfloat16),
        "atom",
        scatter_dimension=0,
        tiled=True,
    )
    reconstruction = rebuilt[:, None, :]
    return (coded_now, reconstruction)


MESH = pl.DeviceIdType.MESH
WIDE = 256
PIECES = 3
LAG = (3, 6, 9, 13)


def dot(a, b, dims):
    return lax.dot_general(a, b, (dims, ((), ())), preferred_element_type=jnp.float32)


def wide(x):
    return x.astype(jnp.float32)


def fused(chunks, tokens, acts, enc_hbm, dec_hbm, thr, codes_out, recon_out,
          enc, dec, own, ends, parts, coded, state, acc, res, terms, core_in, y_out, y_in,
          enc_sem, dec_sem, end_s, end_r, part_s, part_r, code_s, code_s2, code_r,
          a_s, a_r):
    z = lax.axis_index("layer")
    a = lax.axis_index("atom")
    rows = tokens // 4
    core, y = lax.rem(a, 2), a // 2
    mate = a + 1 - 2 * core
    across = lax.rem(a + 2, 4)
    span = acts.shape[1] // PIECES
    is_mid = z * (3 - z) != 0
    is_end = z * (3 - z) == 0

    def load_enc(c):
        return pltpu.make_async_copy(
            enc_hbm.at[:, pl.ds(pl.multiple_of(c * WIDE, WIDE), WIDE)], enc.at[c], enc_sem.at[c])

    def load_dec(c):
        return pltpu.make_async_copy(dec_hbm.at[c], dec.at[c], dec_sem.at[c])

    @pl.loop(0, chunks)
    def _(c):
        load_enc(c).start()

    barrier = pltpu.get_barrier_semaphore()
    for step in (1, 2, 3):
        pl.semaphore_signal(barrier, inc=1, device_id={"layer": lax.rem(z + step, 4)}, device_id_type=MESH)
    for peer in (mate, across):
        pl.semaphore_signal(barrier, inc=1, device_id={"atom": peer}, device_id_type=MESH)
    pl.semaphore_wait(barrier, 5)

    def to_layer(src, dst, send, recv, layer):
        return pltpu.make_async_remote_copy(
            src, dst, send, recv, device_id={"layer": layer}, device_id_type=MESH)

    def to_atom(src, dst, k, atom):
        return pltpu.make_async_remote_copy(
            src, dst, a_s.at[k], a_r.at[k], device_id={"atom": atom}, device_id_type=MESH)

    inner = 1 + z // 3
    outer = 3 * (z - 1)
    other = 3 - z

    def end_copy(c):
        return to_layer(own.at[c], ends.at[c], end_s.at[c], end_r.at[c], inner)

    def part_copy(c):
        return to_layer(own.at[c], parts.at[c], part_s.at[c], part_r.at[c], other)

    def code_out(c):
        return to_layer(coded.at[c], coded.at[c], code_s.at[c], code_r.at[c], outer)

    def code_over(c):
        return to_layer(coded.at[c], coded.at[c], code_s2.at[c], code_r.at[c], other)

    def layer_phase(term, finish, first):
        acc[...] = jnp.zeros_like(acc)

        @pl.loop(0, chunks + LAG[3])
        def _(s):
            @pl.when(s < chunks)
            def _():
                if first:
                    load_dec(s).start()
                own[s] = term(s).astype(jnp.bfloat16)

                @pl.when(is_end)
                def _():
                    end_copy(s).start()

            c1 = s - LAG[0]

            @pl.when(is_mid & (c1 >= 0) & (c1 < chunks))
            def _():
                end_copy(c1).wait_recv()

                @pl.when(z == 2 - lax.rem(c1, 2))
                def _():
                    own[c1] = (wide(own[c1]) + wide(ends[c1])).astype(jnp.bfloat16)
                    part_copy(c1).start()

            c2 = s - LAG[1]

            @pl.when((c2 >= 0) & (c2 < chunks))
            def _():
                @pl.when(z == 1 + lax.rem(c2, 2))
                def _():
                    part_copy(c2).wait_recv()
                    now = finish(c2, wide(own[c2]) + wide(ends[c2]) + wide(parts[c2]))
                    state[c2] = now
                    coded[c2] = now.astype(jnp.bfloat16)
                    code_over(c2).start()
                    code_out(c2).start()

            c3 = s - LAG[2]

            @pl.when((c3 >= 0) & (c3 < chunks))
            def _():
                @pl.when(z == 2 - lax.rem(c3, 2))
                def _():
                    code_over(c3).wait_recv()
                    code_out(c3).start()

            c4 = s - LAG[3]

            @pl.when(c4 >= 0)
            def _():
                @pl.when(is_end)
                def _():
                    code_out(c4).wait_recv()

                if first:
                    load_dec(c4).wait()
                acc[...] += dot(coded[c4], dec[c4], ((1,), (0,)))

        @pl.loop(0, chunks)
        def _(c):
            @pl.when(is_end)
            def _():
                end_copy(c).wait_send()

            @pl.when(is_mid)
            def _():
                code_out(c).wait_send()

            @pl.when(z == 2 - lax.rem(c, 2))
            def _():
                part_copy(c).wait_send()

            @pl.when(z == 1 + lax.rem(c, 2))
            def _():
                code_over(c).wait_send()

    def block(r):
        return pl.ds(pl.multiple_of(r * rows, rows), rows)

    def cols(h):
        return pl.ds(h * span, span)

    def start_sum():
        for r in range(4):
            terms[r] = acc[r * rows:(r + 1) * rows].astype(jnp.bfloat16)
        sent = []
        for h in range(PIECES):
            far = to_atom(terms.at[2 * (1 - y) + 1 - core, :, cols(h)], core_in.at[0, :, cols(h)], 6 * h, mate)
            far.start()
            sent.append([far])
        for h in range(PIECES):
            near = to_atom(terms.at[2 * y + 1 - core, :, cols(h)], core_in.at[1, :, cols(h)], 6 * h + 1, mate)
            near.start()
            sent[h].append(near)
        for h in range(PIECES):
            sent[h][0].wait_recv()
            y_out[:, cols(h)] = (
                wide(terms[2 * (1 - y) + core, :, cols(h)]) + wide(core_in[0, :, cols(h)])
            ).astype(jnp.bfloat16)
            over = to_atom(y_out.at[:, cols(h)], y_in.at[:, cols(h)], 6 * h + 2, across)
            over.start()
            sent[h].append(over)
        return sent

    def piece_sum(sent, h):
        sent[h][1].wait_recv()
        sent[h][2].wait_recv()
        return (wide(terms[2 * y + core, :, cols(h)]) + wide(core_in[1, :, cols(h)])
                + wide(y_in[:, cols(h)]))

    def atom_stage():
        sent = start_sum()
        spread = []
        for h in range(PIECES):
            total = piece_sum(sent, h)
            mine = res.at[block(a), cols(h)]
            theirs = res.at[block(across), cols(h)]
            res[block(a), cols(h)] = (wide(acts[block(a), cols(h)]) - total).astype(jnp.bfloat16)
            over = to_atom(mine, mine, 6 * h + 3, across)
            near = to_atom(mine, mine, 6 * h + 4, mate)
            far = to_atom(theirs, theirs, 6 * h + 5, mate)
            over.start()
            near.start()
            spread.append((over, near, far))
        for over, near, far in spread:
            over.wait_recv()
            far.start()
        for over, near, far in spread:
            near.wait_recv()
            far.wait_recv()
        for h in range(PIECES):
            for copy in sent[h]:
                copy.wait_send()
            for copy in spread[h]:
                copy.wait_send()

    def encode(c):
        load_enc(c).wait()
        return dot(acts[...], enc[c], ((1,), (0,)))

    layer_phase(encode, lambda c, total: jnp.maximum(total - thr[c], 0.0), True)

    def renew():
        acc[...] = jnp.zeros_like(acc)

        @pl.loop(0, chunks)
        def _(c):
            update = dot(coded[c], res[...], ((0,), (0,)))
            dec[c] = (wide(dec[c]) + learn_rate * (update / tokens)).astype(jnp.bfloat16)
            acc[...] += dot(coded[c], dec[c], ((1,), (0,)))

    @pl.loop(0, REFINES + 2)
    def _(p):
        atom_stage()

        @pl.when(p == REFINES)
        def _():
            renew()

        @pl.when(p != REFINES)
        def _():
            layer_phase(
                lambda c: dot(res[...], dec[c], ((1,), (1,))),
                lambda c, total: jnp.maximum(
                    state[c] + step_rate * total - step_rate * thr[c], 0.0),
                False,
            )

    sent = start_sum()
    for c in range(chunks):
        codes_out[:, c * WIDE:(c + 1) * WIDE] = coded[c]
    for h in range(PIECES):
        recon_out[:, cols(h)] = piece_sum(sent, h).astype(jnp.bfloat16)
    for h in range(PIECES):
        for copy in sent[h]:
            copy.wait_send()


def fused_shards(activations, encoder, decoder, thresholds):
    tokens, _, width = activations.shape
    atoms = decoder.shape[0]
    chunks = atoms // WIDE
    rows = tokens // 4
    bf16, f32 = jnp.bfloat16, jnp.float32
    vmem = pl.BlockSpec(memory_space=pltpu.VMEM)
    hbm = pl.BlockSpec(memory_space=pltpu.HBM)
    dma = pltpu.SemaphoreType.DMA
    codes, recon = pl.pallas_call(
        functools.partial(fused, chunks, tokens),
        out_shape=(
            jax.ShapeDtypeStruct((tokens, atoms), bf16),
            jax.ShapeDtypeStruct((rows, width), bf16),
        ),
        in_specs=[vmem, hbm, hbm, vmem],
        out_specs=(vmem, vmem),
        scratch_shapes=[
            pltpu.VMEM((chunks, width, WIDE), bf16),
            pltpu.VMEM((chunks, WIDE, width), bf16),
            pltpu.VMEM((chunks, tokens, WIDE), bf16),
            pltpu.VMEM((chunks, tokens, WIDE), bf16),
            pltpu.VMEM((chunks, tokens, WIDE), bf16),
            pltpu.VMEM((chunks, tokens, WIDE), bf16),
            pltpu.VMEM((chunks, tokens, WIDE), f32),
            pltpu.VMEM((tokens, width), f32),
            pltpu.VMEM((tokens, width), bf16),
            pltpu.VMEM((4, rows, width), bf16),
            pltpu.VMEM((2, rows, width), bf16),
            pltpu.VMEM((rows, width), bf16),
            pltpu.VMEM((rows, width), bf16),
        ] + [dma((chunks,))] * 9 + [dma((6 * PIECES,))] * 2,
        compiler_params=pltpu.CompilerParams(
            collective_id=1, has_side_effects=True, vmem_limit_bytes=60 << 20),
        cost_estimate=pl.CostEstimate(
            flops=20 * tokens * atoms * width, bytes_accessed=4 * atoms * width, transcendentals=0),
        name="crosscoder",
    )(
        activations[:, 0, :],
        encoder[0],
        decoder.reshape(chunks, WIDE, width),
        thresholds.reshape(chunks, 1, WIDE),
    )
    return codes, recon[:, None, :]


def solution(mesh):
    fits = mesh.shape["atom"] == 4 and mesh.shape["layer"] == 4
    return jax.shard_map(
        fused_shards if fits else shards,
        mesh=mesh,
        in_specs=(
            P("group", "layer", None),
            P(("group", "layer"), None, "atom"),
            P(("group", "atom"), "layer", None),
            P(("group", "atom")),
        ),
        out_specs=(P("group", "atom"), P(("group", "atom"), "layer", None)),
        check_vma=False,
    )
```

```python
import functools

import jax
import jax.numpy as jnp
from jax import lax
from jax.experimental import pallas as pl
from jax.experimental.pallas import tpu as pltpu
from jax.sharding import PartitionSpec as P

REFINES = 2


step_rate = 0.15
learn_rate = 0.001


def shards(activations, encoder, decoder, thresholds):
    rows_in = activations[:, 0, :]
    enc_local = encoder[0]
    dec_local = decoder[:, 0, :]
    tokens = rows_in.shape[0]
    atom_devices = lax.axis_size("atom")

    def spread(code_state):
        return code_state.astype(jnp.bfloat16)

    def residual_of(coded_now, weights):
        row_count = tokens // atom_devices
        partial_value = lax.psum_scatter(
            jnp.dot(coded_now, weights, preferred_element_type=jnp.float32).astype(jnp.bfloat16),
            "atom",
            scatter_dimension=0,
            tiled=True,
        ).astype(jnp.float32)
        own_rows = lax.dynamic_slice_in_dim(
            rows_in, lax.axis_index("atom") * row_count, row_count, 0
        ).astype(jnp.float32)
        residual = lax.all_gather(
            (own_rows - partial_value).astype(jnp.bfloat16), "atom", axis=0, tiled=True
        )
        return (residual, False)

    def refine(code_state, coded_now, weights):
        residual, transposed = residual_of(coded_now, weights)
        gradient = lax.psum(
            lax.dot_general(
                residual, weights, (((1,), (1,)), ((), ())), preferred_element_type=jnp.float32
            ).astype(jnp.bfloat16),
            "layer",
        ).astype(jnp.float32)
        code_state = jax.nn.relu(code_state + step_rate * gradient - step_rate * thresholds)
        return (code_state, spread(code_state))

    preact = lax.psum(
        jnp.dot(rows_in, enc_local, preferred_element_type=jnp.float32).astype(jnp.bfloat16),
        "layer",
    ).astype(jnp.float32)
    code_state = jax.nn.relu(preact - thresholds)
    coded_now = spread(code_state)
    for sweep in range(REFINES):
        code_state, coded_now = refine(code_state, coded_now, dec_local)
    residual, transposed = residual_of(coded_now, dec_local)
    update = lax.dot_general(
        coded_now, residual, (((0,), (0,)), ((), ())), preferred_element_type=jnp.float32
    )
    renewed = (dec_local.astype(jnp.float32) + learn_rate * (update / tokens)).astype(jnp.bfloat16)
    code_state, coded_now = refine(code_state, coded_now, renewed)
    rebuilt = lax.psum_scatter(
        jnp.dot(coded_now, renewed, preferred_element_type=jnp.float32).astype(jnp.bfloat16),
        "atom",
        scatter_dimension=0,
        tiled=True,
    )
    reconstruction = rebuilt[:, None, :]
    return (coded_now, reconstruction)


MESH = pl.DeviceIdType.MESH
WIDE = 256
PIECES = 3
LAG = (3, 6, 9, 13)


def dot(a, b, dims):
    return lax.dot_general(a, b, (dims, ((), ())), preferred_element_type=jnp.float32)


def wide(x):
    return x.astype(jnp.float32)


def fused(chunks, tokens, acts, enc_hbm, dec_hbm, thr, codes_out, recon_out,
          enc, dec, own, ends, parts, coded, state, acc, res, terms, core_in, y_out, y_in,
          enc_sem, dec_sem, end_s, end_r, part_s, part_r, code_s, code_s2, code_r,
          a_s, a_r):
    z = lax.axis_index("layer")
    a = lax.axis_index("atom")
    rows = tokens // 4
    core, y = lax.rem(a, 2), a // 2
    mate = a + 1 - 2 * core
    across = lax.rem(a + 2, 4)
    span = acts.shape[1] // PIECES
    is_mid = z * (3 - z) != 0
    is_end = z * (3 - z) == 0

    def load_enc(c):
        return pltpu.make_async_copy(
            enc_hbm.at[:, pl.ds(pl.multiple_of(c * WIDE, WIDE), WIDE)], enc.at[c], enc_sem.at[c])

    def load_dec(c):
        return pltpu.make_async_copy(dec_hbm.at[c], dec.at[c], dec_sem.at[c])

    @pl.loop(0, chunks)
    def _(c):
        load_enc(c).start()

    barrier = pltpu.get_barrier_semaphore()
    for step in (1, 2, 3):
        pl.semaphore_signal(barrier, inc=1, device_id={"layer": lax.rem(z + step, 4)}, device_id_type=MESH)
    for peer in (mate, across):
        pl.semaphore_signal(barrier, inc=1, device_id={"atom": peer}, device_id_type=MESH)
    pl.semaphore_wait(barrier, 5)

    def to_layer(src, dst, send, recv, layer):
        return pltpu.make_async_remote_copy(
            src, dst, send, recv, device_id={"layer": layer}, device_id_type=MESH)

    def to_atom(src, dst, k, atom):
        return pltpu.make_async_remote_copy(
            src, dst, a_s.at[k], a_r.at[k], device_id={"atom": atom}, device_id_type=MESH)

    inner = 1 + z // 3
    outer = 3 * (z - 1)
    other = 3 - z

    def end_copy(c):
        return to_layer(own.at[c], ends.at[c], end_s.at[c], end_r.at[c], inner)

    def part_copy(c):
        return to_layer(own.at[c], parts.at[c], part_s.at[c], part_r.at[c], other)

    def code_out(c):
        return to_layer(coded.at[c], coded.at[c], code_s.at[c], code_r.at[c], outer)

    def code_over(c):
        return to_layer(coded.at[c], coded.at[c], code_s2.at[c], code_r.at[c], other)

    def layer_phase(term, finish, first):
        acc[...] = jnp.zeros_like(acc)

        @pl.loop(0, chunks + LAG[3])
        def _(s):
            @pl.when(s < chunks)
            def _():
                if first:
                    load_dec(s).start()
                own[s] = term(s).astype(jnp.bfloat16)

                @pl.when(is_end)
                def _():
                    end_copy(s).start()

            c1 = s - LAG[0]

            @pl.when(is_mid & (c1 >= 0) & (c1 < chunks))
            def _():
                end_copy(c1).wait_recv()

                @pl.when(z == 2 - lax.rem(c1, 2))
                def _():
                    own[c1] = (wide(own[c1]) + wide(ends[c1])).astype(jnp.bfloat16)
                    part_copy(c1).start()

            c2 = s - LAG[1]

            @pl.when((c2 >= 0) & (c2 < chunks))
            def _():
                @pl.when(z == 1 + lax.rem(c2, 2))
                def _():
                    part_copy(c2).wait_recv()
                    now = finish(c2, wide(own[c2]) + wide(ends[c2]) + wide(parts[c2]))
                    state[c2] = now
                    coded[c2] = now.astype(jnp.bfloat16)
                    code_over(c2).start()
                    code_out(c2).start()

            c3 = s - LAG[2]

            @pl.when((c3 >= 0) & (c3 < chunks))
            def _():
                @pl.when(z == 2 - lax.rem(c3, 2))
                def _():
                    code_over(c3).wait_recv()
                    code_out(c3).start()

            c4 = s - LAG[3]

            @pl.when(c4 >= 0)
            def _():
                @pl.when(is_end)
                def _():
                    code_out(c4).wait_recv()

                if first:
                    load_dec(c4).wait()
                acc[...] += dot(coded[c4], dec[c4], ((1,), (0,)))

        @pl.loop(0, chunks)
        def _(c):
            @pl.when(is_end)
            def _():
                end_copy(c).wait_send()

            @pl.when(is_mid)
            def _():
                code_out(c).wait_send()

            @pl.when(z == 2 - lax.rem(c, 2))
            def _():
                part_copy(c).wait_send()

            @pl.when(z == 1 + lax.rem(c, 2))
            def _():
                code_over(c).wait_send()

    def block(r):
        return pl.ds(pl.multiple_of(r * rows, rows), rows)

    def cols(h):
        return pl.ds(h * span, span)

    def start_sum():
        for r in range(4):
            terms[r] = acc[r * rows:(r + 1) * rows].astype(jnp.bfloat16)
        sent = []
        for h in range(PIECES):
            far = to_atom(terms.at[2 * (1 - y) + 1 - core, :, cols(h)], core_in.at[0, :, cols(h)], 6 * h, mate)
            far.start()
            sent.append([far])
        for h in range(PIECES):
            near = to_atom(terms.at[2 * y + 1 - core, :, cols(h)], core_in.at[1, :, cols(h)], 6 * h + 1, mate)
            near.start()
            sent[h].append(near)
        for h in range(PIECES):
            sent[h][0].wait_recv()
            y_out[:, cols(h)] = (
                wide(terms[2 * (1 - y) + core, :, cols(h)]) + wide(core_in[0, :, cols(h)])
            ).astype(jnp.bfloat16)
            over = to_atom(y_out.at[:, cols(h)], y_in.at[:, cols(h)], 6 * h + 2, across)
            over.start()
            sent[h].append(over)
        return sent

    def piece_sum(sent, h):
        sent[h][1].wait_recv()
        sent[h][2].wait_recv()
        return (wide(terms[2 * y + core, :, cols(h)]) + wide(core_in[1, :, cols(h)])
                + wide(y_in[:, cols(h)]))

    def atom_stage():
        sent = start_sum()
        spread = []
        for h in range(PIECES):
            total = piece_sum(sent, h)
            mine = res.at[block(a), cols(h)]
            theirs = res.at[block(across), cols(h)]
            res[block(a), cols(h)] = (wide(acts[block(a), cols(h)]) - total).astype(jnp.bfloat16)
            over = to_atom(mine, mine, 6 * h + 3, across)
            near = to_atom(mine, mine, 6 * h + 4, mate)
            far = to_atom(theirs, theirs, 6 * h + 5, mate)
            over.start()
            near.start()
            spread.append((over, near, far))
        for over, near, far in spread:
            over.wait_recv()
            far.start()
        for over, near, far in spread:
            near.wait_recv()
            far.wait_recv()
        for h in range(PIECES):
            for copy in sent[h]:
                copy.wait_send()
            for copy in spread[h]:
                copy.wait_send()

    def encode(c):
        load_enc(c).wait()
        return dot(acts[...], enc[c], ((1,), (0,)))

    layer_phase(encode, lambda c, total: jnp.maximum(total - thr[c], 0.0), True)

    def renew():
        acc[...] = jnp.zeros_like(acc)

        @pl.loop(0, chunks, unroll=2)
        def _(c):
            update = dot(coded[c], res[...], ((0,), (0,)))
            dec[c] = (wide(dec[c]) + update * (learn_rate / tokens)).astype(jnp.bfloat16)
            acc[...] += dot(coded[c], dec[c], ((1,), (0,)))

    @pl.loop(0, REFINES + 2)
    def _(p):
        atom_stage()

        @pl.when(p == REFINES)
        def _():
            renew()

        @pl.when(p != REFINES)
        def _():
            layer_phase(
                lambda c: dot(res[...], dec[c], ((1,), (1,))),
                lambda c, total: jnp.maximum(
                    state[c] + step_rate * total - step_rate * thr[c], 0.0),
                False,
            )

    sent = start_sum()
    for c in range(chunks):
        codes_out[:, c * WIDE:(c + 1) * WIDE] = coded[c]
    for h in range(PIECES):
        recon_out[:, cols(h)] = piece_sum(sent, h).astype(jnp.bfloat16)
    for h in range(PIECES):
        for copy in sent[h]:
            copy.wait_send()


def fused_shards(activations, encoder, decoder, thresholds):
    tokens, _, width = activations.shape
    atoms = decoder.shape[0]
    chunks = atoms // WIDE
    rows = tokens // 4
    bf16, f32 = jnp.bfloat16, jnp.float32
    vmem = pl.BlockSpec(memory_space=pltpu.VMEM)
    hbm = pl.BlockSpec(memory_space=pltpu.HBM)
    dma = pltpu.SemaphoreType.DMA
    codes, recon = pl.pallas_call(
        functools.partial(fused, chunks, tokens),
        out_shape=(
            jax.ShapeDtypeStruct((tokens, atoms), bf16),
            jax.ShapeDtypeStruct((rows, width), bf16),
        ),
        in_specs=[vmem, hbm, hbm, vmem],
        out_specs=(vmem, vmem),
        scratch_shapes=[
            pltpu.VMEM((chunks, width, WIDE), bf16),
            pltpu.VMEM((chunks, WIDE, width), bf16),
            pltpu.VMEM((chunks, tokens, WIDE), bf16),
            pltpu.VMEM((chunks, tokens, WIDE), bf16),
            pltpu.VMEM((chunks, tokens, WIDE), bf16),
            pltpu.VMEM((chunks, tokens, WIDE), bf16),
            pltpu.VMEM((chunks, tokens, WIDE), f32),
            pltpu.VMEM((tokens, width), f32),
            pltpu.VMEM((tokens, width), bf16),
            pltpu.VMEM((4, rows, width), bf16),
            pltpu.VMEM((2, rows, width), bf16),
            pltpu.VMEM((rows, width), bf16),
            pltpu.VMEM((rows, width), bf16),
        ] + [dma((chunks,))] * 9 + [dma((6 * PIECES,))] * 2,
        compiler_params=pltpu.CompilerParams(
            collective_id=1, has_side_effects=True, vmem_limit_bytes=60 << 20),
        cost_estimate=pl.CostEstimate(
            flops=20 * tokens * atoms * width, bytes_accessed=4 * atoms * width, transcendentals=0),
        name="crosscoder",
    )(
        activations[:, 0, :],
        encoder[0],
        decoder.reshape(chunks, WIDE, width),
        thresholds.reshape(chunks, 1, WIDE),
    )
    return codes, recon[:, None, :]


def solution(mesh):
    fits = mesh.shape["atom"] == 4 and mesh.shape["layer"] == 4
    return jax.shard_map(
        fused_shards if fits else shards,
        mesh=mesh,
        in_specs=(
            P("group", "layer", None),
            P(("group", "layer"), None, "atom"),
            P(("group", "atom"), "layer", None),
            P(("group", "atom")),
        ),
        out_specs=(P("group", "atom"), P(("group", "atom"), "layer", None)),
        check_vma=False,
    )
```
